32 devices in a mesh: seq: 8 (over z, core), fsdp: 4 (over y, x).
Axes of the slice: x: 2, y: 2, z: 4, core: 2. Of those that a mesh axis runs over, the one named last changes fastest.
Arguments:
- tokens: bfloat16 [4, 1024, 4096], P('fsdp', 'seq'), may hold values from -40 to 40
- cotangent: bfloat16 [4, 1024, 4096], P('fsdp', 'seq'), may hold values from -6 to 6
- w_query: bfloat16 [4096, 2048], P(None, 'fsdp'), may hold values from -0.09375 to 0.09375
- w_key: bfloat16 [4096, 2048], P(None, 'fsdp'), may hold values from -0.09375 to 0.09375
- w_value: bfloat16 [4096, 2048], P(None, 'fsdp'), may hold values from -0.09375 to 0.09375
- w_output: bfloat16 [2048, 4096], P('fsdp'), may hold values from -0.125 to 0.125
- global_pos: int32 [4, 128], replicated, may hold values from 0 to 1023
- pattern: int32 [4, 16, 2], P(None, 'seq'), may hold values 0 or 1
Outputs:
- grad_tokens: bfloat16 [4, 1024, 4096], P('fsdp', 'seq')
- grad_query: float32 [4096, 2048], P('seq', 'fsdp')
- grad_key: float32 [4096, 2048], P('seq', 'fsdp')
- grad_value: float32 [4096, 2048], P('seq', 'fsdp')
- grad_output: float32 [2048, 4096], P('fsdp', 'seq')
The draws below stay inside these ranges and needn't reach their ends.
All inputs are finite; a program needn't handle non-finite values. No bound on the sum of `pattern` on one device may be relied on, other than what follows from the above.
Results may differ from the reference program's by a relative error of at most 0.019.
Values may be sent and summed in bfloat16 or wider, within the bound.
No kernel may reach another device: no remote copies, remote signals or barrier semaphores. Data moves between devices by JAX's collectives and lax.ppermute only.
A program may use at most 192 MiB of HBM per device.

```python
import jax
import jax.numpy as jnp
from jax import lax

D = 4096
HEADS = 16
HDIM = 128
BLOCK = 64
NGLOB = 128
TOK_DEV = 128
DOCUMENT_COUNT = 4
SEQUENCE_LENGTH = 1024
NBLOCKS = 16
N_SEQ = 8
N_FSDP = 4


def draw_tokens(key, part):
    key = jax.random.fold_in(key, 11)
    first_key = jax.random.fold_in(key, 0)
    dims_shape = (DOCUMENT_COUNT, SEQUENCE_LENGTH, D)
    value_rows = jax.random.normal(first_key, dims_shape, jnp.float32)
    return jnp.clip(value_rows, -40.0, 40.0).astype(jnp.bfloat16)


def touch_ends(drawn, rng, least, top_value):
    spot = [jax.random.randint(jax.random.fold_in(rng, axis), (), 0, length) for axis, length in enumerate(drawn.shape)]
    longest = drawn.shape.index(max(drawn.shape))
    next_to = spot[:longest] + [(spot[longest] + 1) % drawn.shape[longest]] + spot[longest + 1:]
    return drawn.at[tuple(spot)].set(least).at[tuple(next_to)].set(top_value)


def steps_of(key, extent, shards, least, high):
    level = 1.0
    for position, parts in shards:
        steps = jax.random.uniform(jax.random.fold_in(jax.random.fold_in(key, 6), position), (parts,), jnp.float32, least / len(shards), high / len(shards))
        level = level * jnp.repeat(jnp.exp(steps), extent[position] // parts).reshape((-1,) + (1,) * (len(extent) - 1 - position))
    return level


def noise(key, extent, width, reach, cuts=(), kind=jnp.bfloat16):
    level = steps_of(key, extent, cuts, -0.22, 0.18) if cuts else 1.0
    values = jax.random.normal(key, extent, jnp.float32) * width * level
    return jnp.minimum(jnp.maximum(values, -reach), reach).astype(kind)


def setup_inputs(seed: int = 0) -> dict:
    key_of = jax.random.split(jax.random.key(seed), 9)
    tokens = draw_tokens(jax.random.fold_in(key_of[8], 71), 0)
    cotangent = noise(key_of[1], (DOCUMENT_COUNT, SEQUENCE_LENGTH, D), 1.0, 6.0, ((0, 4), (1, 8)))
    w_query = noise(key_of[2], (D, HEADS * HDIM), D ** -0.5, 0.09375, ((1, 4),))
    w_key = noise(key_of[3], (D, HEADS * HDIM), D ** -0.5, 0.09375, ((1, 4),))
    w_value = noise(key_of[4], (D, HEADS * HDIM), D ** -0.5, 0.09375, ((1, 4),))
    w_output = noise(key_of[5], (HEADS * HDIM, D), (HEADS * HDIM) ** -0.5, 0.125, ((0, 4),))
    global_pos = touch_ends(jax.random.randint(key_of[6], (DOCUMENT_COUNT, NGLOB), 0, SEQUENCE_LENGTH), jax.random.fold_in(key_of[6], 1), 0, SEQUENCE_LENGTH - 1).astype(jnp.int32)
    pattern = touch_ends((jax.random.randint(key_of[7], (DOCUMENT_COUNT, NBLOCKS, 2), 0, 4) < 3).astype(jnp.int32), jax.random.fold_in(key_of[7], 1), 0, 1)
    return {"tokens": tokens, "cotangent": cotangent, "w_query": w_query, "w_key": w_key, "w_value": w_value, "w_output": w_output, "global_pos": global_pos, "pattern": pattern}


def product(form, left, right):
    return jnp.einsum(form, left.astype(jnp.float32), right.astype(jnp.float32))


def block_mask(pattern, first_block, block_total):
    block_count = pattern.shape[0]
    index = first_block + jnp.arange(block_count, dtype=jnp.int32)
    before = (pattern[:, 0] == 1) & (index > 0)
    after = (pattern[:, 1] == 1) & (index < block_total - 1)
    middle = jnp.ones((block_count, BLOCK), jnp.bool_)
    return jnp.concatenate([jnp.broadcast_to(before[:, None], (block_count, BLOCK)), middle,
                            jnp.broadcast_to(after[:, None], (block_count, BLOCK))], axis=1)


def windows(extended, block_count):
    blocks = extended.reshape(block_count + 2, BLOCK, extended.shape[-1])
    return jnp.concatenate([blocks[:block_count], blocks[1:block_count + 1], blocks[2:]], axis=1)


def unwindow(grads, block_count):
    lower = grads[:, :BLOCK]
    center = grads[:, BLOCK:2 * BLOCK]
    upper = grads[:, 2 * BLOCK:]
    summed = jnp.pad(lower, ((0, 2), (0, 0), (0, 0))) + jnp.pad(center, ((1, 1), (0, 0), (0, 0)))
    summed = summed + jnp.pad(upper, ((2, 0), (0, 0), (0, 0)))
    return summed.reshape((block_count + 2) * BLOCK, grads.shape[-1])


def doc_attention(query, extended, global_kv, pattern, grad_ctx, first_block, block_total):
    row_count, head_width = query.shape
    block_count = row_count // BLOCK
    head_count = head_width // HDIM
    scale = HDIM ** -0.5
    window_kv = windows(extended, block_count)
    key_win = window_kv[..., :head_width].reshape(block_count, 3 * BLOCK, head_count, HDIM)
    value_win = window_kv[..., head_width:].reshape(block_count, 3 * BLOCK, head_count, HDIM)
    key_glob = global_kv[:, :head_width].reshape(-1, head_count, HDIM)
    value_glob = global_kv[:, head_width:].reshape(-1, head_count, HDIM)
    queries = query.reshape(block_count, BLOCK, head_count, HDIM)
    grad_out = grad_ctx.reshape(block_count, BLOCK, head_count, HDIM)
    mask = block_mask(pattern, first_block, block_total)
    local = product('nqhe,nkhe->nhqk', queries, key_win) * scale
    local = jnp.where(mask[:, None, None, :], local, -jnp.inf)
    remote = product('nqhe,ghe->nhqg', queries, key_glob) * scale
    top = jnp.maximum(local.max(-1), remote.max(-1))[..., None]
    local_exp = jnp.exp(local - top)
    remote_exp = jnp.exp(remote - top)
    denom = local_exp.sum(-1, keepdims=True) + remote_exp.sum(-1, keepdims=True)
    p_local = local_exp / denom
    p_remote = remote_exp / denom
    p_local_b = p_local.astype(jnp.bfloat16)
    p_remote_b = p_remote.astype(jnp.bfloat16)
    context = (product('nhqk,nkhe->nqhe', p_local_b, value_win)
               + product('nhqg,ghe->nqhe', p_remote_b, value_glob)).astype(jnp.bfloat16)
    d_local = product('nqhe,nkhe->nhqk', grad_out, value_win)
    d_remote = product('nqhe,ghe->nhqg', grad_out, value_glob)
    delta = (p_local * d_local).sum(-1, keepdims=True) + (p_remote * d_remote).sum(-1, keepdims=True)
    s_local = (p_local * (d_local - delta) * scale).astype(jnp.bfloat16)
    s_remote = (p_remote * (d_remote - delta) * scale).astype(jnp.bfloat16)
    grad_q = (product('nhqk,nkhe->nqhe', s_local, key_win)
              + product('nhqg,ghe->nqhe', s_remote, key_glob)).astype(jnp.bfloat16)
    dkey_win = product('nhqk,nqhe->nkhe', s_local, queries)
    dvalue_win = product('nhqk,nqhe->nkhe', p_local_b, grad_out)
    dkey_glob = product('nhqg,nqhe->ghe', s_remote, queries)
    dvalue_glob = product('nhqg,nqhe->ghe', p_remote_b, grad_out)
    grad_ext = unwindow(jnp.concatenate([dkey_win.reshape(block_count, 3 * BLOCK, head_width),
                                         dvalue_win.reshape(block_count, 3 * BLOCK, head_width)], -1), block_count)
    grad_glob = jnp.concatenate([dkey_glob.reshape(-1, head_width), dvalue_glob.reshape(-1, head_width)], -1)
    return context.reshape(row_count, head_width), grad_q.reshape(row_count, head_width), grad_ext, grad_glob


def contract_rows(left, right):
    return lax.dot_general(left, right, (((0,), (0,)), ((), ())), preferred_element_type=jnp.float32)


def contract_cols(left, right):
    return lax.dot_general(left, right, (((1,), (1,)), ((), ())), preferred_element_type=jnp.float32)


def reference(tokens, cotangent, w_query, w_key, w_value, w_output, global_pos, pattern):
    head_width = HEADS * HDIM
    flat = tokens.reshape(-1, D)
    query = jnp.dot(flat, w_query, preferred_element_type=jnp.float32).astype(jnp.bfloat16)
    keys = jnp.dot(flat, w_key, preferred_element_type=jnp.float32).astype(jnp.bfloat16)
    value_rows = jnp.dot(flat, w_value, preferred_element_type=jnp.float32).astype(jnp.bfloat16)
    grads_flat = cotangent.reshape(-1, D)
    grad_ctx = contract_cols(grads_flat, w_output).astype(jnp.bfloat16)

    def per_doc(items):
        doc_query, doc_keys, doc_values, doc_grad, doc_pos, doc_pattern = items
        keys_vals = jnp.concatenate([doc_keys, doc_values], -1)
        extended = jnp.pad(keys_vals, ((BLOCK, BLOCK), (0, 0)))
        global_kv = jnp.take(keys_vals, doc_pos, axis=0)
        context, grad_q, grad_ext, grad_glob = doc_attention(doc_query, extended, global_kv, doc_pattern,
                                                             doc_grad, 0, NBLOCKS)
        owned = grad_ext[BLOCK:-BLOCK].at[doc_pos].add(grad_glob)
        return (context, grad_q, owned[:, :head_width].astype(jnp.bfloat16),
                owned[:, head_width:].astype(jnp.bfloat16))

    def shaped(array):
        return array.reshape(DOCUMENT_COUNT, SEQUENCE_LENGTH, head_width)

    context, grad_q, grad_k, grad_v = lax.map(per_doc, (shaped(query), shaped(keys), shaped(value_rows),
                                                        shaped(grad_ctx), global_pos, pattern))
    flat_q = grad_q.reshape(-1, head_width)
    flat_k = grad_k.reshape(-1, head_width)
    flat_v = grad_v.reshape(-1, head_width)
    group = head_width // N_FSDP
    grad_sum = jnp.zeros((DOCUMENT_COUNT * SEQUENCE_LENGTH, D), jnp.float32)
    for index in range(N_FSDP):
        lo_col = index * group
        hi_col = lo_col + group
        term = (contract_cols(flat_q[:, lo_col:hi_col], w_query[:, lo_col:hi_col])
                + contract_cols(flat_k[:, lo_col:hi_col], w_key[:, lo_col:hi_col])
                + contract_cols(flat_v[:, lo_col:hi_col], w_value[:, lo_col:hi_col]))
        grad_sum = grad_sum + term.astype(jnp.bfloat16).astype(jnp.float32)
    grad_tokens = grad_sum.astype(jnp.bfloat16).reshape(DOCUMENT_COUNT, SEQUENCE_LENGTH, D)

    def shard_term(accum, shard):
        begin = shard * TOK_DEV

        def take(array):
            return lax.dynamic_slice_in_dim(array, begin, TOK_DEV, 1).reshape(DOCUMENT_COUNT * TOK_DEV, array.shape[-1])

        inputs = take(tokens)
        grads_in = take(cotangent)
        term = jnp.concatenate([contract_rows(inputs, take(grad_q)), contract_rows(inputs, take(grad_k)),
                                contract_rows(inputs, take(grad_v)), contract_rows(grads_in, take(context))], 1)
        return accum + term.astype(jnp.bfloat16).astype(jnp.float32), None

    accum, unused = lax.scan(shard_term, jnp.zeros((D, 4 * head_width), jnp.float32),
                             jnp.arange(N_SEQ, dtype=jnp.int32))
    grad_query = accum[:, :head_width]
    grad_key = accum[:, head_width:2 * head_width]
    grad_value = accum[:, 2 * head_width:3 * head_width]
    grad_output = accum[:, 3 * head_width:].T
    return grad_tokens, grad_query, grad_key, grad_value, grad_output
```

```python
import functools

import jax
import jax.numpy as jnp
from jax import lax
from jax.experimental import pallas as pl
from jax.experimental.pallas import tpu as pltpu
from jax.sharding import PartitionSpec as P

HDIM = 128
BLOCK = 64
LOW = -1e30
CORES = 2
TILE = 256
BF16 = jnp.bfloat16
F32 = jnp.float32


def swap(value, axis, mask):
    return lax.ppermute(value, axis, [(i, i ^ mask) for i in range(lax.axis_size(axis))])


def near_indices(count):
    return [1 << k for k in range(count.bit_length() - 1)]


def near_blocks(block, axis):
    return {r: swap(block, axis, r) for r in near_indices(lax.axis_size(axis))}


def far_blocks(halves, axis):
    count = lax.axis_size(axis)
    halves = dict(halves)
    for r in sorted(set(range(1, count)) - set(halves), key=lambda i: (bin(i).count("1"), i)):
        low, high = r & -r, 1 << (r.bit_length() - 1)
        halves[r] = (swap(halves[r ^ low][0], axis, low), swap(halves[r ^ high][1], axis, high))
    return halves


def cut(block):
    half = block.shape[0] // 2
    return block[:half], block[half:]


def phase(tree):
    return lax.optimization_barrier(tree)


class BlockScatter:
    def __init__(self, terms, axis):
        self.axis = axis
        self.terms = {r: [[piece] for piece in pieces] for r, pieces in terms.items()}

    def add(self, pieces):
        total = pieces[0]
        if len(pieces) > 1:
            total = pieces[0].astype(F32)
            for piece in pieces[1:]:
                total = total + piece.astype(F32)
        return total

    def send(self, weight):
        for r in [r for r in self.terms if bin(r).count("1") == weight]:
            ways = [r & -r, 1 << (r.bit_length() - 1)]
            for k, pieces in enumerate(self.terms[r]):
                value = swap(self.add(pieces).astype(BF16), self.axis, ways[k])
                there = self.terms[r ^ ways[k]]
                if weight > 2 or weight == 1:
                    there[k if weight > 2 else 0].append(value)
                else:
                    missing = jnp.zeros_like(value)
                    there[0].append(jnp.concatenate([value, missing] if k == 0 else [missing, value], 0))
            del self.terms[r]

    def collapse(self):
        for halves in self.terms.values():
            for pieces in halves:
                pieces[:] = [self.add(pieces).astype(BF16)]

    def own(self):
        return [pieces[0] for halves in self.terms.values() for pieces in halves]

    def put_own(self, values):
        for pieces in [pieces for halves in self.terms.values() for pieces in halves]:
            pieces[0] = values.pop(0)

    def total(self):
        return self.add(self.terms[0][0])


def halves_of(value, upper):
    half = value.shape[0] // 2
    mine = lax.dynamic_slice_in_dim(value, upper * half, half, 0)
    return mine, lax.dynamic_slice_in_dim(value, (1 - upper) * half, half, 0)


def sum_first(mine, other, chip):
    mine, other = halves_of(mine + swap(other, "seq", 1), chip & 1)
    return mine + swap(other, "seq", CORES)


def sum_second(value, chips):
    for k in range(1, chips.bit_length() - 1):
        last = swap(value, "seq", CORES << k)
        if k < chips.bit_length() - 2:
            value = value + last
    return value, last


def sum_third(value, chip):
    other = swap(value, "seq", CORES)
    return jnp.where(
        chip & 1 == 1, jnp.concatenate([other, value], 0), jnp.concatenate([value, other], 0)
    )


def sum_last(mine, core):
    other = swap(mine, "seq", 1)
    return jnp.where(core == 0, mine, other), jnp.where(core == 0, other, mine)


def shift_pairs(count, step):
    return [(i, i + step) for i in range(count) if 0 <= i + step < count]


def contract_rows(left, right):
    return lax.dot_general(left, right, (((0,), (0,)), ((), ())), preferred_element_type=F32)


def contract_cols(left, right):
    return lax.dot_general(left, right, (((1,), (1,)), ((), ())), preferred_element_type=F32)


RESIDENT = pl.BlockSpec(memory_space=pltpu.VMEM)


def resident(value):
    return pltpu.with_memory_space_constraint(value, pltpu.VMEM), RESIDENT


def fixed(shape):
    return pl.BlockSpec(shape, lambda *unused: (0,) * len(shape))


def call(kernel, grid, scalars, ins, outs, flops, limit=16, scratch=(), space=pltpu.HBM, free=()):
    return pl.pallas_call(
        kernel,
        grid_spec=pltpu.PrefetchScalarGridSpec(
            num_scalar_prefetch=1,
            grid=grid,
            in_specs=[spec for _, spec in ins],
            out_specs=[spec for _, _, spec in outs],
            scratch_shapes=scratch,
        ),
        out_shape=[space(shape, dtype) for shape, dtype, _ in outs],
        compiler_params=pltpu.CompilerParams(vmem_limit_bytes=limit << 20),
        cost_estimate=pl.CostEstimate(flops=flops >> 8, bytes_accessed=1024, transcendentals=0),
    )(
        scalars,
        *[a if k in free or spec is RESIDENT else pltpu.with_memory_space_constraint(a, pltpu.HBM) for k, (a, spec) in enumerate(ins)],
    )


def accumulate(total_ref, term):
    @pl.when(pl.program_id(0) == 0)
    def _():
        total_ref[...] = term

    @pl.when(pl.program_id(0) > 0)
    def _():
        total_ref[...] += term


def fill(parts, flat_ref):
    start = 0
    for part in parts:
        flat_ref[start : start + part.shape[0]] = part[...]
        start += part.shape[0]


def keys_kernel(tiles, docs, core_ref, *refs):
    *parts, sel_ref, wk_ref, wv_ref = refs[:-7]
    k_ref, v_ref, first_ref, last_ref, mine_ref, other_ref, flat_ref = refs[-7:]
    step, core = pl.program_id(0), core_ref[0]

    @pl.when(step == 0)
    def _():
        fill(parts, flat_ref)

    def emit(weight_ref, out_ref, owner):
        out = jnp.dot(flat_ref[...], weight_ref[...], preferred_element_type=F32).astype(BF16)
        out_ref[...] = out
        rows = out.shape[0] // docs
        globs = sel_ref.shape[0] // docs
        picked = []
        for doc in range(docs):
            part = out[doc * rows : (doc + 1) * rows]
            first_ref[doc * BLOCK : (doc + 1) * BLOCK] = part[:BLOCK]
            last_ref[doc * BLOCK : (doc + 1) * BLOCK] = part[rows - BLOCK :]
            chosen = sel_ref[doc * globs : (doc + 1) * globs]
            picked.append(jnp.dot(chosen, part, preferred_element_type=F32).astype(BF16))

        @pl.when(core == owner)
        def _():
            for doc in range(docs):
                mine_ref[doc * globs : (doc + 1) * globs] = picked[doc]

        @pl.when(core != owner)
        def _():
            for doc in range(docs):
                other_ref[doc * globs : (doc + 1) * globs] = picked[doc]

    @pl.when(step < tiles)
    def _():
        emit(wk_ref, k_ref, 0)

    @pl.when(step >= tiles)
    def _():
        emit(wv_ref, v_ref, 1)


def project_keys(parts, selector, w_key, w_value, core, docs):
    rows = sum(p.shape[0] for p in parts)
    depth, width = w_key.shape
    tile = min(TILE, width // 2)
    tiles = width // tile
    low = lambda i, *_: (0, jnp.minimum(i, tiles - 1))
    high = lambda i, *_: (0, jnp.maximum(i - tiles, 0))
    each = lambda i, *_: (0, i)
    share = lambda owner: lambda i, c: (
        0, jnp.clip(i - tiles * jnp.where(c[0] == owner, 0, 1), 0, tiles - 1)
    )
    globs = selector.shape[0]
    edge = docs * BLOCK
    return call(
        functools.partial(keys_kernel, tiles, docs),
        (2 * tiles,),
        core.reshape(1),
        [resident(p) for p in parts]
        + [(selector, fixed(selector.shape))]
        + [(w_key, pl.BlockSpec((depth, tile), low)), (w_value, pl.BlockSpec((depth, tile), high))],
        [
            ((rows, width), BF16, pl.BlockSpec((rows, tile), low)),
            ((rows, width), BF16, pl.BlockSpec((rows, tile), high)),
            ((edge, 2 * width), BF16, pl.BlockSpec((edge, tile), each)),
            ((edge, 2 * width), BF16, pl.BlockSpec((edge, tile), each)),
            ((globs, width), BF16, pl.BlockSpec((globs, tile), share(0))),
            ((globs, width), BF16, pl.BlockSpec((globs, tile), share(1))),
        ],
        4 * rows * depth * width,
        limit=(rows + 4 * tile) * depth * 2 // 2**20 + 8,
        scratch=[pltpu.VMEM((rows, depth), BF16)],
    )


def project_kernel(flip, tiles, slices, core_ref, *refs):
    *parts, w_ref = refs[:-4]
    flat_ref, send_ref, out_ref, whole_ref = refs[-4:]
    step, core = pl.program_id(0), core_ref[0]
    size = whole_ref.shape[1] // slices

    @pl.when(step == 0)
    def _():
        fill(parts, whole_ref)

    for index in range(tiles):

        @pl.when(step == index)
        def _(index=index):
            if flip:
                out_ref[...] = contract_cols(whole_ref[...], w_ref[...]).astype(BF16)
            else:
                out = jnp.dot(whole_ref[...], w_ref[...], preferred_element_type=F32)
                out_ref[...] = out.astype(BF16)
            wide = flat_ref.shape[1]
            flat_ref[...] = whole_ref[:, index * wide : (index + 1) * wide]
            for k in range(slices // CORES // tiles):
                shard = CORES * (index * (slices // CORES // tiles) + k)
                begin = pl.multiple_of((shard + CORES - 1 - core) * size, size)
                send_ref[:, k * size : (k + 1) * size] = whole_ref[:, pl.ds(begin, size)]


def project(parts, weight, core, slices, flip):
    rows = sum(p.shape[0] for p in parts)
    depth, width = weight.shape[::-1] if flip else weight.shape
    tile = min(TILE, width // 2)
    tiles = width // tile
    each = lambda i, *_: (0, i)
    return call(
        functools.partial(project_kernel, flip, tiles, slices),
        (tiles,),
        core.reshape(1),
        [(p, fixed(p.shape)) if flip else resident(p) for p in parts]
        + [(weight, pl.BlockSpec((tile, depth), lambda i, *_: (i, 0)) if flip else pl.BlockSpec((depth, tile), each))],
        [
            ((rows, depth), BF16, pl.BlockSpec((rows, depth // tiles), each)),
            ((rows, depth // CORES), BF16, pl.BlockSpec((rows, depth // CORES // tiles), each)),
            ((rows, width), BF16, pl.BlockSpec((rows, tile), each)),
        ],
        2 * rows * depth * width,
        limit=((rows * (tiles + 3) // tiles + 2 * tile) + 2 * rows * flip) * depth * 2 // 2**20 + 5,
        scratch=[pltpu.VMEM((rows, depth), BF16)],
    )


def key_mask(flags_ref, doc, rows, total):
    row_block = lax.broadcasted_iota(jnp.int32, (rows, total), 0) // BLOCK
    col = lax.broadcasted_iota(jnp.int32, (rows, total), 1)
    offset = col // BLOCK - row_block
    seen = (offset == 1) | (col >= rows + 2 * BLOCK)
    window = col < rows + 2 * BLOCK
    for block in range(rows // BLOCK):
        here = (row_block == block) & window
        before = flags_ref[doc, 2 * block] == 1
        past = flags_ref[doc, 2 * block + 1] == 1
        seen = seen | (here & (offset == 0) & before) | (here & (offset == 2) & past)
    return seen


def joined(before_ref, own_ref, after_ref, glob_ref, head, shift):
    cols = slice(head * HDIM, (head + 1) * HDIM)
    side = slice(shift + head * HDIM, shift + (head + 1) * HDIM)
    return jnp.concatenate(
        [before_ref[:, side], own_ref[:, cols], after_ref[:, side], glob_ref[:, cols]], 0
    )


def attention_kernel(
    flags_ref, q_ref, k_ref, v_ref, before_ref, after_ref, gk_ref, gv_ref, do_ref,
    ctx_ref, dq_ref, dk_ref, dv_ref, dbefore_ref, dafter_ref, mine_ref, other_ref,
):
    rows, width = q_ref.shape
    total = rows + 2 * BLOCK + gk_ref.shape[0]
    doc = pl.program_id(0)
    seen = key_mask(flags_ref, doc, rows, total)
    first_core = flags_ref[doc, 2 * (rows // BLOCK)] == 0
    heads = range(width // HDIM)
    cols = [slice(head * HDIM, (head + 1) * HDIM) for head in heads]
    keys = [joined(before_ref, k_ref, after_ref, gk_ref, head, 0) for head in heads]
    values = [joined(before_ref, v_ref, after_ref, gv_ref, head, width) for head in heads]
    scores = [contract_cols(q_ref[:, cols[h]], keys[h]) * HDIM**-0.5 for h in heads]
    dweights = [contract_cols(do_ref[:, cols[h]], values[h]) for h in heads]
    scores = [jnp.where(seen, s, LOW) for s in scores]
    tops = [s.max(-1, keepdims=True) for s in scores]
    grown = [jnp.exp(scores[h] - tops[h]) for h in heads]
    sums = [g.sum(-1, keepdims=True) for g in grown]
    weights = [grown[h] / sums[h] for h in heads]
    deltas = [(weights[h] * dweights[h]).sum(-1, keepdims=True) for h in heads]
    weights_b = [w.astype(BF16) for w in weights]
    for h in heads:
        ctx_ref[:, cols[h]] = jnp.dot(weights_b[h], values[h], preferred_element_type=F32).astype(BF16)
    dvalues = [contract_rows(weights_b[h], do_ref[:, cols[h]]) for h in heads]
    dscores = [
        (weights[h] * (dweights[h] - deltas[h]) * HDIM**-0.5).astype(BF16) for h in heads
    ]
    for h in heads:
        dq_ref[:, cols[h]] = jnp.dot(dscores[h], keys[h], preferred_element_type=F32).astype(BF16)
    dkeys = [contract_rows(dscores[h], q_ref[:, cols[h]]) for h in heads]
    for h in heads:
        for own_ref, shift, grads in ((dk_ref, 0, dkeys[h]), (dv_ref, width, dvalues[h])):
            side = slice(shift + h * HDIM, shift + (h + 1) * HDIM)
            own_ref[:, cols[h]] = grads[BLOCK : rows + BLOCK]
            dbefore_ref[:, side] = grads[:BLOCK].astype(BF16)
            dafter_ref[:, side] = grads[rows + BLOCK : rows + 2 * BLOCK].astype(BF16)
        gk, gv = dkeys[h][rows + 2 * BLOCK :], dvalues[h][rows + 2 * BLOCK :]
        mine_ref[:, cols[h]] = jnp.where(first_core, gk, gv).astype(BF16)
        other_ref[:, cols[h]] = jnp.where(first_core, gv, gk).astype(BF16)


def by_doc(rows, width):
    return pl.BlockSpec((rows, width), lambda doc, *unused: (doc, 0))


def attention(kernel, docs, flags, operands, out_rows, flops, free):
    return call(
        kernel,
        (docs,),
        flags,
        [(a, by_doc(a.shape[0] // docs, a.shape[1])) for a in operands],
        [((docs * rows, width), dtype, by_doc(rows, width)) for rows, width, dtype in out_rows],
        flops,
        free=free,
    )


def finish_kernel(
    core_ref, dq_ref, dk_ref, dv_ref, ctx_ref, before_ref, after_ref, keys_ref, values_ref
):
    rows, width = dk_ref.shape
    keys_ref[:, :width] = dq_ref[...]
    values_ref[:, :width] = ctx_ref[...]
    cols = slice(width, 2 * width)
    for own_ref, shift, out_ref in ((dk_ref, 0, keys_ref), (dv_ref, width, values_ref)):
        side = slice(shift, shift + width)
        out_ref[:BLOCK, cols] = (own_ref[:BLOCK] + before_ref[:, side].astype(F32)).astype(BF16)
        if rows > 2 * BLOCK:
            out_ref[BLOCK : rows - BLOCK, cols] = own_ref[BLOCK : rows - BLOCK].astype(BF16)
        out_ref[rows - BLOCK :, cols] = (own_ref[rows - BLOCK :] + after_ref[:, side].astype(F32)).astype(BF16)


def whole_kernel(
    core_ref, dk_ref, dv_ref, before_ref, after_ref, gk_ref, gv_ref, sel_ref, k_ref, v_ref
):
    rows, width = dk_ref.shape
    for own_ref, glob_ref, shift, out_ref in ((dk_ref, gk_ref, 0, k_ref), (dv_ref, gv_ref, width, v_ref)):
        total = own_ref[...] + contract_rows(sel_ref[...], glob_ref[...])
        side = slice(shift, shift + width)
        out_ref[:BLOCK] = (total[:BLOCK] + before_ref[:, side].astype(F32)).astype(BF16)
        if rows > 2 * BLOCK:
            out_ref[BLOCK : rows - BLOCK] = total[BLOCK : rows - BLOCK].astype(BF16)
        out_ref[rows - BLOCK :] = (total[rows - BLOCK :] + after_ref[:, side].astype(F32)).astype(BF16)


def transposed(value):
    return value.astype(F32).T.astype(value.dtype)


def terms_kernel(core_ref, c_ref, csib_ref, x_ref, xsib_ref, g_ref, gsib_ref, out_ref, turned_ref):
    rows, width = g_ref.shape[0], g_ref.shape[1] // 2
    size = x_ref.shape[1]

    @pl.when(pl.program_id(0) == 0)
    def _():
        turned_ref[:, :rows] = transposed(g_ref[...])
        turned_ref[:, rows:] = transposed(gsib_ref[...])

    for k, (own_ref, sib_ref) in enumerate(((c_ref, csib_ref), (x_ref, xsib_ref))):
        both = jnp.concatenate([own_ref[...], sib_ref[...]], 0)
        out = jnp.dot(turned_ref[k * width : (k + 1) * width], both, preferred_element_type=F32)
        out_ref[0, :, k * size : (k + 1) * size] = out.astype(BF16)


def chip_terms(cots, tokens, grads, core, slices):
    rows, depth = cots[0].shape
    width = grads.shape[1] // 2
    size, chips = depth // slices, slices // CORES
    own = pl.BlockSpec((rows, size), lambda z, c: (0, CORES * z + c[0]))
    other = pl.BlockSpec((rows, size), lambda z, c: (0, z))
    return call(
        terms_kernel,
        (chips,),
        core.reshape(1),
        [
            (cots[0], own),
            (cots[1], other),
            (tokens[0], own),
            (tokens[1], other),
            (grads, fixed(grads.shape)),
            (swap(grads, "seq", 1), fixed(grads.shape)),
        ],
        [((chips, width, 2 * size), BF16, pl.BlockSpec((1, width, 2 * size), lambda z, c: (z, 0, 0)))],
        8 * rows * size * chips * width,
        limit=24,
        scratch=[pltpu.VMEM((2 * width, 2 * rows), BF16)],
    )[0]


def line_schedule(count):
    return [
        {
            c: ("all", c - step) if step <= c else ("sum", count + c - step)
            for c in range(count - 1)
        }
        for step in range(count)
    ]


def pieces_kernel(count, table_ref, right_ref, left_ref, *refs):
    for way, (own_ref, out_ref) in enumerate(((right_ref, refs[-2]), (left_ref, refs[-1]))):
        is_sum, begins = table_ref[3 * way + 1] == 1, table_ref[3 * way + 2] == 1
        begin = 0
        for came_ref in refs[way * count : (way + 1) * count]:
            here = slice(begin, begin + came_ref.shape[1])
            begin += came_ref.shape[1]
            own, came = own_ref[0, :, here], came_ref[...]
            added = (own.astype(F32) + came.astype(F32)).astype(BF16)
            out_ref[:, here] = jnp.where(is_sum, jnp.where(begins, own, added), came)


def lookup(place, values):
    result = jnp.int32(values[0])
    for k, value in enumerate(values[1:], 1):
        result = jnp.where(place == k, jnp.int32(value), result)
    return result


class Line:
    def __init__(self, shape, chip, chips):
        self.partial, self.chip, self.chips, self.shape = None, chip, chips, shape
        self.schedule = line_schedule(chips)
        self.values, self.firsts, self.received = [], [], []

    def begin(self, value):
        self.values.append(value)
        self.firsts.append(self.move((value, value)))

    def join(self):
        self.rows, self.wide = self.values[0].shape[0], sum(v.shape[1] for v in self.values)
        self.size = tuple(max(a, b) for a, b in zip((self.rows, self.wide), self.shape))
        self.received.append(tuple(self.fit(jnp.concatenate(way, 1)) for way in zip(*self.firsts)))

    def fit(self, value):
        missing = [(0, want - have) for want, have in zip(self.size, value.shape)]
        return jnp.pad(value, missing) if any(m for _, m in missing) else value

    def place(self, sign):
        return self.chip if sign > 0 else self.chips - 1 - self.chip

    def pieces(self):
        chosen, pieces, table = self.schedule[len(self.received)], [], []
        count = self.chips
        plain = len(self.firsts) > 1 and len(self.received) == 1 and self.size == self.shape == (self.rows, self.wide)
        for way, sign in enumerate((1, -1)):
            place = self.place(sign)
            sums = [int(chosen.get(c, ("", 0))[0] == "sum") for c in range(count)]
            which = [chosen.get(c, ("", c))[1] for c in range(count)]
            to = lookup(place, which)
            to = to if sign > 0 else count - 1 - to
            if plain:
                table += [to, lookup(place, sums), (place == 0).astype(jnp.int32)]
                continue
            own = self.fit(lax.dynamic_index_in_dim(self.partial, to, 0, keepdims=False))
            before = self.received[-1][way]
            added = (own.astype(F32) + before.astype(F32)).astype(BF16)
            pieces.append(jnp.where(lookup(place, sums) == 1, jnp.where(place == 0, own, added), before))
        if not plain:
            return pieces
        arrived = [list(way) for way in zip(*self.firsts)]
        rows, wide = self.size
        part = rows // 4
        return call(
            functools.partial(pieces_kernel, len(arrived[0])),
            (4,),
            jnp.stack(table),
            [(self.partial, pl.BlockSpec((1, part, wide), lambda i, t, at=at: (t[at], i, 0))) for at in (0, 3)]
            + [(a, pl.BlockSpec((part, a.shape[1]), lambda i, *_: (i, 0))) for way in arrived for a in way],
            [((rows, wide), BF16, pl.BlockSpec((part, wide), lambda i, *_: (i, 0)))] * 2,
            0,
            space=jax.ShapeDtypeStruct,
            free=range(2, 8),
        )

    def move(self, pieces):
        count, got = self.chips, []
        for piece, sign in zip(pieces, (1, -1)):
            pairs = [
                (c * CORES + b, (c + sign) * CORES + b)
                for c in (range(count - 1) if sign > 0 else range(count - 1, 0, -1))
                for b in range(CORES)
            ]
            got.append(lax.ppermute(piece, "seq", pairs))
        return tuple(got)

    def send(self, pieces):
        self.received.append(self.move(pieces))

    def step(self):
        self.send(self.pieces())

    def gathered(self, columns, sums, positions, core):
        rows, wide = self.rows, self.wide
        slots, grads = [jnp.int32(0)], [self.values]
        for t in range(self.chips - 1):
            for way, sign in enumerate((1, -1)):
                values = [-1] * self.chips
                for c, (kind, which) in self.schedule[t].items():
                    if kind == "all":
                        values[c + 1] = (sign * (c + 1 - which)) % self.chips
                slots.append(lookup(self.place(sign), values))
                if t:
                    grads.append([self.received[t][way][:rows, :wide]])
                else:
                    grads.append([first[way] for first in self.firsts])
        height, width = columns[0].shape[1], wide // 2
        size = height // CORES
        once = lambda a: (a, pl.BlockSpec(a.shape, lambda *_: (0,) * a.ndim, pipeline_mode=pl.Buffered(1)))
        return call(
            functools.partial(gathered_kernel, len(columns), [len(g) for g in grads]),
            (1,),
            jnp.stack(slots + [core, self.chip]),
            [once(a) for a in columns + list(sums) + [positions] + sum(grads, [])],
            [
                ((size, 3 * width), F32, fixed((size, 3 * width))),
            ]
            + [((size, width), BF16, fixed((size, width)))] * 3,
            4 * height * width * len(grads) * rows,
            limit=44,
            scratch=[pltpu.VMEM((height, 3 * width), F32)],
        )


def final_kernel(
    chip_ref, terms_ref, right_ref, left_ref, mine_ref, *refs
):
    others, (q_ref, k_ref, v_ref, o_ref) = refs[:3], refs[3:]
    width, size = q_ref.shape[1], o_ref.shape[1]
    rows, wide = terms_ref.shape[1:]
    summed = terms_ref[0].astype(F32)
    summed += right_ref[:rows, :wide].astype(F32)
    summed += left_ref[:rows, :wide].astype(F32)
    o_ref[...] = summed[:, :size]
    q_ref[...] = mine_ref[:, :width] + others[0][...].astype(F32)
    k_ref[...] = mine_ref[:, width : 2 * width] + others[1][...].astype(F32)
    v_ref[...] = mine_ref[:, 2 * width :] + others[2][...].astype(F32) + summed[:, size:].T


def final_sums(line, mine, others, width):
    _, rows, wide = line.partial.shape
    size = mine.shape[0]
    return call(
        final_kernel,
        (1,),
        line.chip.reshape(1),
        [(line.partial, pl.BlockSpec((1, rows, wide), lambda i, c: (c[0], 0, 0)))]
        + [(a, fixed(a.shape)) for a in (*line.received[-1], mine, *others)],
        [((size, width), F32, fixed((size, width)))] * 3 + [((rows, size), F32, fixed((rows, size)))],
        0,
        limit=32,
        free=range(1, 7),
    )


def columns_to_chips(block, chip, chips):
    turned = block.T
    size = turned.shape[0] // chips
    pieces = []
    for s in range(chips):
        piece = lax.dynamic_slice_in_dim(turned, lax.rem(chip + s, chips) * size, size, 0)
        if s:
            pairs = [
                (c * CORES + b, (c + s) % chips * CORES + b) for c in range(chips) for b in range(CORES)
            ]
            piece = lax.ppermute(piece, "seq", pairs)
        pieces.append(piece)
    return pieces


def gathered_kernel(docs, groups, slots_ref, *refs):
    x_refs, (gk_ref, gv_ref, positions_ref), g_refs = refs[:docs], refs[docs : docs + 3], refs[docs + 3 : -5]
    mine_ref, *other_refs, total_ref = refs[-5:]
    width = gk_ref.shape[1]
    sent = 2 * width
    chips, _, rows = x_refs[0].shape
    core, chip = slots_ref[len(groups)], slots_ref[len(groups) + 1]

    def add(slot, group, first):
        x = jnp.concatenate([x_ref[slot] for x_ref in x_refs], 1)
        begin = 0
        for g_ref in group:
            here = slice(begin, begin + g_ref.shape[1])
            term = jnp.dot(x, g_ref[...], preferred_element_type=F32)
            total_ref[:, here] = term if first else total_ref[:, here] + term
            begin += g_ref.shape[1]

    begin = 0
    for k, count in enumerate(groups):
        group = g_refs[begin : begin + count]
        begin += count
        if k == 0:
            add(0, group, True)
            continue

        @pl.when(slots_ref[k] >= 0)
        def _(k=k, group=group):
            add(slots_ref[k], group, False)

    globs = gk_ref.shape[0] // docs
    chosen = []
    for doc in range(docs):
        picked = None
        for slot in range(chips):
            begin = (lax.rem(chip + chips - slot, chips) * CORES + core) * rows
            place = begin + lax.broadcasted_iota(jnp.int32, (rows, globs), 0)
            onehot = (place == positions_ref[doc]).astype(F32).astype(BF16)
            part = jnp.dot(x_refs[doc][slot], onehot, preferred_element_type=F32)
            picked = part if picked is None else picked + part
        chosen.append(picked.astype(BF16))
    chosen = jnp.concatenate(chosen, 1)
    total_ref[:, sent - width : sent] += jnp.dot(chosen, gk_ref[...], preferred_element_type=F32)
    total_ref[:, sent:] = jnp.dot(chosen, gv_ref[...], preferred_element_type=F32)

    size = mine_ref.shape[0]
    mine_ref[...] = total_ref[pl.ds(pl.multiple_of(core * size, size), size)]
    other = total_ref[pl.ds(pl.multiple_of((CORES - 1 - core) * size, size), size)]
    for k, other_ref in enumerate(other_refs):
        other_ref[...] = other[:, k * width : (k + 1) * width].astype(BF16)


def tokens_kernel(places, core_ref, q_ref, k_ref, v_ref, wq_ref, wk_ref, wv_ref, *out_refs):
    total = None
    for g_ref, w_ref in ((q_ref, wq_ref), (k_ref, wk_ref), (v_ref, wv_ref)):
        term = contract_cols(w_ref[...], g_ref[...])
        total = term if total is None else total + term
    total = total.T.astype(BF16)
    for (begin, count), out_ref in zip(places, out_refs):
        out_ref[...] = total[begin : begin + count]


def token_terms(docs, rows, grads, weights, core):
    depth, width = weights[0].shape
    tile = 512
    places = []
    for r in range(docs):
        halves = 2 if bin(r).count("1") > 1 else 1
        places += [(r * rows + k * rows // halves, rows // halves) for k in range(halves)]
    pieces = call(
        functools.partial(tokens_kernel, places),
        (depth // tile,),
        core.reshape(1),
        [(g, fixed(g.shape)) for g in grads]
        + [(w, pl.BlockSpec((tile, width), lambda i, *_: (i, 0))) for w in weights],
        [((count, depth), BF16, pl.BlockSpec((count, tile), lambda i, *_: (0, i))) for _, count in places],
        6 * docs * rows * depth * width,
        limit=24,
    )
    terms = {r: [] for r in range(docs)}
    for (begin, _), piece in zip(places, pieces):
        terms[begin // rows].append(piece)
    return terms


def on_device(tokens, cotangent, w_query, w_key, w_value, w_output, global_pos, pattern):
    docs = lax.axis_size("fsdp")
    n_seq = lax.axis_size("seq")
    seq = lax.axis_index("seq")
    core, chip, chips = lax.rem(seq, CORES), lax.div(seq, CORES), n_seq // CORES
    rows, model_width = tokens.shape[1:]
    width = w_query.shape[1]
    block_count = rows // BLOCK
    order = lax.axis_index("fsdp") ^ jnp.arange(docs, dtype=jnp.int32)
    global_pos = jnp.take(global_pos, order, axis=0)
    pattern = jnp.take(pattern, order, axis=0)
    globs = global_pos.shape[1]

    index = seq * block_count + jnp.arange(block_count, dtype=jnp.int32)
    inside = jnp.stack([index > 0, index < block_count * n_seq - 1], -1)
    flags = ((pattern == 1) & inside[None]).astype(jnp.int32).reshape(docs, 2 * block_count)
    flags = jnp.concatenate([flags, jnp.broadcast_to(core, (docs, 1))], 1)
    selector = (
        (global_pos[:, :, None] - seq * rows == jnp.arange(rows, dtype=jnp.int32)[None, None, :])
        .astype(BF16)
        .reshape(docs * globs, rows)
    )

    block, cot = tokens[0], cotangent[0]
    pieces = columns_to_chips(block, chip, chips)
    near, selector, flags = phase((near_blocks(block, "fsdp"), selector, flags))
    whole = {0: block, **near}
    far = far_blocks({r: cut(v) for r, v in whole.items()}, "fsdp")
    parts = [p for r in range(docs) for p in ([whole[r]] if r in whole else far[r])]
    parts, cot_halves, pieces = phase((parts, cut(cot), pieces))

    near_a = near_blocks(cot_halves[0], "fsdp")
    keys, values, first, last, mine, other = project_keys(
        parts, selector, w_key, w_value, core, docs
    )
    keys, values, first, last, mine, other, near_a, cot_b, parts, pieces = phase(
        (keys, values, first, last, mine, other, near_a, cot_halves[1], parts, pieces)
    )

    near_b = near_blocks(cot_b, "fsdp")
    glob = sum_first(mine, other, chip)
    flat, for_sibling, query = project(parts, w_query, core, n_seq, False)
    glob, near_b, flat, query, for_sibling, first, last, pieces = phase(
        (glob, near_b, flat, query, for_sibling, first, last, pieces)
    )
    halves = {0: (cot_halves[0], cot_b)}
    halves.update({r: (near_a[r], near_b[r]) for r in near_a})
    far = far_blocks(halves, "fsdp")
    glob = sum(sum_second(glob, chips))
    columns = jnp.stack(pieces)
    glob, far, first, last, for_sibling, columns = phase((glob, far, first, last, for_sibling, columns))
    glob = sum_third(glob, chip)
    past = lax.ppermute(first, "seq", shift_pairs(n_seq, -1))
    before = lax.ppermute(last, "seq", shift_pairs(n_seq, 1))
    cot_parts = [cot] + [p for r in range(1, docs) for p in far[r]]
    grads_flat, grads_for_sibling, grad_ctx = project(cot_parts, w_output, core, n_seq, True)
    glob, grads_flat, grads_for_sibling, grad_ctx, columns, for_sibling, past, before = phase(
        (glob, grads_flat, grads_for_sibling, grad_ctx, columns, for_sibling, past, before)
    )
    glob_k, glob_v = sum_last(glob, core)
    glob_k, glob_v, grads_for_sibling, for_sibling = phase(
        (glob_k, glob_v, grads_for_sibling, for_sibling)
    )
    grads_sibling = swap(grads_for_sibling, "seq", 1)
    tokens_sibling = swap(for_sibling, "seq", 1)

    near_columns = near_blocks(columns, "fsdp")
    context, grad_q, dkey, dvalue, dbefore, dafter, dmine, dother = attention(
        attention_kernel,
        docs,
        flags,
        [query, keys, values, before, past, glob_k, glob_v, grad_ctx],
        [
            (rows, width, BF16),
            (rows, width, BF16),
            (rows, width, F32),
            (rows, width, F32),
            (BLOCK, 2 * width, BF16),
            (BLOCK, 2 * width, BF16),
            (globs, width, BF16),
            (globs, width, BF16),
        ],
        14 * docs * rows * (rows + 2 * BLOCK + globs) * width,
        free=(3, 4, 5, 6),
    )

    (context, grad_q, dkey, dvalue, dbefore, dafter, dmine, dother), columns, grads_sibling, tokens_sibling = phase(
        ((context, grad_q, dkey, dvalue, dbefore, dafter, dmine, dother), columns, grads_sibling, tokens_sibling)
    )

    line = Line((width, 2 * model_width // n_seq), chip, chips)
    kept, given = halves_of(dmine + swap(dother, "seq", 1), chip & 1)
    kept, given, dbefore, dafter, grad_q = phase((kept, given, dbefore, dafter, grad_q))
    given = swap(given, "seq", CORES)
    from_after = lax.ppermute(dbefore, "seq", shift_pairs(n_seq, -1))
    from_before = lax.ppermute(dafter, "seq", shift_pairs(n_seq, 1))
    dglob, context = phase((kept + given, context))
    dglob, came = sum_second(dglob, chips)
    to_gather, to_scatter = call(
        finish_kernel,
        (docs,),
        core.reshape(1),
        [
            (a, by_doc(a.shape[0] // docs, a.shape[1]))
            for a in (grad_q, dkey, dvalue, context, from_before, from_after)
        ],
        [((docs * rows, 2 * width), BF16, by_doc(rows, 2 * width))] * 2,
        4 * docs * rows * globs * width,
        free=(4, 5),
    )
    to_gather, to_scatter, columns, near_columns, came = phase(
        (to_gather, to_scatter, columns, near_columns, came)
    )
    dglob = dglob + came

    line.begin(to_gather)
    line.partial = chip_terms((grads_flat, grads_sibling), (flat, tokens_sibling), to_scatter, core, n_seq)
    line.firsts, line.partial, dglob = phase((line.firsts, line.partial, dglob))
    line.join()
    line.step()
    dglob = sum_third(dglob, chip)
    whole = {0: columns, **near_columns}
    far = far_blocks({r: cut(v) for r, v in whole.items()}, "fsdp")
    sums = sum_last(dglob, core)
    grad_k, grad_v = call(
        whole_kernel,
        (docs,),
        core.reshape(1),
        [
            (a, by_doc(a.shape[0] // docs, a.shape[1]))
            for a in (dkey, dvalue, from_before, from_after, *sums, selector)
        ],
        [((docs * rows, width), BF16, by_doc(rows, width))] * 2,
        4 * docs * rows * globs * width,
        free=(4, 5),
    )
    terms = token_terms(docs, rows, (grad_q, grad_k, grad_v), (w_query, w_key, w_value), core)
    line.received, sums, far, whole, terms = phase((line.received, sums, far, whole, terms))
    scatter, bits = BlockScatter(terms, "fsdp"), docs.bit_length() - 1
    pieces, far, own_terms = phase((line.pieces(), far, scatter.own()))
    scatter.put_own(own_terms)
    line.send(pieces)
    columns = [whole[r] if r in whole else jnp.concatenate(far[r], 0) for r in range(docs)]
    scatter.send(bits)
    scatter.collapse()
    line.received, sums, columns, scatter.terms = phase((line.received, sums, columns, scatter.terms))
    while len(line.received) < len(line.schedule) - 1:
        line.step()
    pieces, sums, columns, own_terms = phase((line.pieces(), sums, columns, scatter.own()))
    scatter.put_own(own_terms)
    line.send(pieces)
    for weight in range(bits - 1, 0, -1):
        scatter.send(weight)
    mine, *others = line.gathered(columns, sums, global_pos[:, None, :], core)
    grad_tokens, others = phase((scatter.total().astype(BF16)[None], others))
    others = [swap(other, "seq", 1) for other in others]
    line.received, mine, others = phase((line.received, mine, others))
    grad_query, grad_key, grad_value, grad_output = final_sums(line, mine, others, width)
    return (grad_tokens, grad_query, grad_key, grad_value, grad_output)


def solution(mesh):
    in_specs = (
        P("fsdp", "seq", None),
        P("fsdp", "seq", None),
        P(None, "fsdp"),
        P(None, "fsdp"),
        P(None, "fsdp"),
        P("fsdp", None),
        P(),
        P(None, "seq", None),
    )
    out_specs = (
        P("fsdp", "seq", None),
        P("seq", "fsdp"),
        P("seq", "fsdp"),
        P("seq", "fsdp"),
        P("fsdp", "seq"),
    )
    return jax.shard_map(
        on_device, mesh=mesh, in_specs=in_specs, out_specs=out_specs, check_vma=False
    )
```

```python
import functools

import jax
import jax.numpy as jnp
from jax import lax
from jax.experimental import pallas as pl
from jax.experimental.pallas import tpu as pltpu
from jax.sharding import PartitionSpec as P

HDIM = 128
BLOCK = 64
LOW = -1e30
CORES = 2
TILE = 256
BF16 = jnp.bfloat16
F32 = jnp.float32


def swap(value, axis, mask):
    return lax.ppermute(value, axis, [(i, i ^ mask) for i in range(lax.axis_size(axis))])


def near_indices(count):
    return [1 << k for k in range(count.bit_length() - 1)]


def near_blocks(block, axis):
    return {r: swap(block, axis, r) for r in near_indices(lax.axis_size(axis))}


def far_blocks(halves, axis):
    count = lax.axis_size(axis)
    halves = dict(halves)
    for r in sorted(set(range(1, count)) - set(halves), key=lambda i: (bin(i).count("1"), i)):
        low, high = r & -r, 1 << (r.bit_length() - 1)
        halves[r] = (swap(halves[r ^ low][0], axis, low), swap(halves[r ^ high][1], axis, high))
    return halves


def cut(block):
    half = block.shape[0] // 2
    return block[:half], block[half:]


def phase(tree):
    return lax.optimization_barrier(tree)


class BlockScatter:
    def __init__(self, terms, axis):
        self.axis = axis
        self.terms = {r: [[piece] for piece in pieces] for r, pieces in terms.items()}

    def add(self, pieces):
        total = pieces[0]
        if len(pieces) > 1:
            total = pieces[0].astype(F32)
            for piece in pieces[1:]:
                total = total + piece.astype(F32)
        return total

    def send(self, weight):
        for r in [r for r in self.terms if bin(r).count("1") == weight]:
            ways = [r & -r, 1 << (r.bit_length() - 1)]
            for k, pieces in enumerate(self.terms[r]):
                value = swap(self.add(pieces).astype(BF16), self.axis, ways[k])
                there = self.terms[r ^ ways[k]]
                if weight > 2 or weight == 1:
                    there[k if weight > 2 else 0].append(value)
                else:
                    missing = jnp.zeros_like(value)
                    there[0].append(jnp.concatenate([value, missing] if k == 0 else [missing, value], 0))
            del self.terms[r]

    def collapse(self):
        for halves in self.terms.values():
            for pieces in halves:
                pieces[:] = [self.add(pieces).astype(BF16)]

    def own(self):
        return [pieces[0] for halves in self.terms.values() for pieces in halves]

    def put_own(self, values):
        for pieces in [pieces for halves in self.terms.values() for pieces in halves]:
            pieces[0] = values.pop(0)

    def total(self):
        return self.add(self.terms[0][0])


def halves_of(value, upper):
    half = value.shape[0] // 2
    mine = lax.dynamic_slice_in_dim(value, upper * half, half, 0)
    return mine, lax.dynamic_slice_in_dim(value, (1 - upper) * half, half, 0)


def sum_first(mine, other, chip):
    mine, other = halves_of(mine + swap(other, "seq", 1), chip & 1)
    return mine + swap(other, "seq", CORES)


def sum_second(value, chips):
    for k in range(1, chips.bit_length() - 1):
        last = swap(value, "seq", CORES << k)
        if k < chips.bit_length() - 2:
            value = value + last
    return value, last


def sum_third(value, chip):
    other = swap(value, "seq", CORES)
    return jnp.where(
        chip & 1 == 1, jnp.concatenate([other, value], 0), jnp.concatenate([value, other], 0)
    )


def sum_last(mine, core):
    other = swap(mine, "seq", 1)
    return jnp.where(core == 0, mine, other), jnp.where(core == 0, other, mine)


def shift_pairs(count, step):
    return [(i, i + step) for i in range(count) if 0 <= i + step < count]


def contract_rows(left, right):
    return lax.dot_general(left, right, (((0,), (0,)), ((), ())), preferred_element_type=F32)


def contract_cols(left, right):
    return lax.dot_general(left, right, (((1,), (1,)), ((), ())), preferred_element_type=F32)


RESIDENT = pl.BlockSpec(memory_space=pltpu.VMEM)


def resident(value):
    return pltpu.with_memory_space_constraint(value, pltpu.VMEM), RESIDENT


def fixed(shape):
    return pl.BlockSpec(shape, lambda *unused: (0,) * len(shape))


def call(kernel, grid, scalars, ins, outs, flops, limit=16, scratch=(), space=pltpu.HBM, free=()):
    return pl.pallas_call(
        kernel,
        grid_spec=pltpu.PrefetchScalarGridSpec(
            num_scalar_prefetch=1,
            grid=grid,
            in_specs=[spec for _, spec in ins],
            out_specs=[spec for _, _, spec in outs],
            scratch_shapes=scratch,
        ),
        out_shape=[space(shape, dtype) for shape, dtype, _ in outs],
        compiler_params=pltpu.CompilerParams(vmem_limit_bytes=limit << 20),
        cost_estimate=pl.CostEstimate(flops=flops >> 8, bytes_accessed=1024, transcendentals=0),
    )(
        scalars,
        *[a if k in free or spec is RESIDENT else pltpu.with_memory_space_constraint(a, pltpu.HBM) for k, (a, spec) in enumerate(ins)],
    )


def accumulate(total_ref, term):
    @pl.when(pl.program_id(0) == 0)
    def _():
        total_ref[...] = term

    @pl.when(pl.program_id(0) > 0)
    def _():
        total_ref[...] += term


def fill(parts, flat_ref):
    start = 0
    for part in parts:
        flat_ref[start : start + part.shape[0]] = part[...]
        start += part.shape[0]


def keys_kernel(tiles, docs, core_ref, *refs):
    *parts, sel_ref, wk_ref, wv_ref = refs[:-7]
    k_ref, v_ref, first_ref, last_ref, mine_ref, other_ref, flat_ref = refs[-7:]
    step, core = pl.program_id(0), core_ref[0]

    @pl.when(step == 0)
    def _():
        fill(parts, flat_ref)

    def emit(weight_ref, out_ref, owner):
        out = jnp.dot(flat_ref[...], weight_ref[...], preferred_element_type=F32).astype(BF16)
        out_ref[...] = out
        rows = out.shape[0] // docs
        globs = sel_ref.shape[0] // docs
        picked = []
        for doc in range(docs):
            part = out[doc * rows : (doc + 1) * rows]
            first_ref[doc * BLOCK : (doc + 1) * BLOCK] = part[:BLOCK]
            last_ref[doc * BLOCK : (doc + 1) * BLOCK] = part[rows - BLOCK :]
            chosen = sel_ref[doc * globs : (doc + 1) * globs]
            picked.append(jnp.dot(chosen, part, preferred_element_type=F32).astype(BF16))

        @pl.when(core == owner)
        def _():
            for doc in range(docs):
                mine_ref[doc * globs : (doc + 1) * globs] = picked[doc]

        @pl.when(core != owner)
        def _():
            for doc in range(docs):
                other_ref[doc * globs : (doc + 1) * globs] = picked[doc]

    @pl.when(step < tiles)
    def _():
        emit(wk_ref, k_ref, 0)

    @pl.when(step >= tiles)
    def _():
        emit(wv_ref, v_ref, 1)


def project_keys(parts, selector, w_key, w_value, core, docs):
    rows = sum(p.shape[0] for p in parts)
    depth, width = w_key.shape
    tile = min(TILE, width // 2)
    tiles = width // tile
    low = lambda i, *_: (0, jnp.minimum(i, tiles - 1))
    high = lambda i, *_: (0, jnp.maximum(i - tiles, 0))
    each = lambda i, *_: (0, i)
    share = lambda owner: lambda i, c: (
        0, jnp.clip(i - tiles * jnp.where(c[0] == owner, 0, 1), 0, tiles - 1)
    )
    globs = selector.shape[0]
    edge = docs * BLOCK
    return call(
        functools.partial(keys_kernel, tiles, docs),
        (2 * tiles,),
        core.reshape(1),
        [resident(p) for p in parts]
        + [(selector, fixed(selector.shape))]
        + [(w_key, pl.BlockSpec((depth, tile), low)), (w_value, pl.BlockSpec((depth, tile), high))],
        [
            ((rows, width), BF16, pl.BlockSpec((rows, tile), low)),
            ((rows, width), BF16, pl.BlockSpec((rows, tile), high)),
            ((edge, 2 * width), BF16, pl.BlockSpec((edge, tile), each)),
            ((edge, 2 * width), BF16, pl.BlockSpec((edge, tile), each)),
            ((globs, width), BF16, pl.BlockSpec((globs, tile), share(0))),
            ((globs, width), BF16, pl.BlockSpec((globs, tile), share(1))),
        ],
        4 * rows * depth * width,
        limit=(rows + 4 * tile) * depth * 2 // 2**20 + 8,
        scratch=[pltpu.VMEM((rows, depth), BF16)],
    )


def project_kernel(flip, tiles, slices, core_ref, *refs):
    *parts, w_ref = refs[:-4]
    flat_ref, send_ref, out_ref, whole_ref = refs[-4:]
    step, core = pl.program_id(0), core_ref[0]
    size = whole_ref.shape[1] // slices

    @pl.when(step == 0)
    def _():
        fill(parts, whole_ref)

    for index in range(tiles):

        @pl.when(step == index)
        def _(index=index):
            if flip:
                out_ref[...] = contract_cols(whole_ref[...], w_ref[...]).astype(BF16)
            else:
                out = jnp.dot(whole_ref[...], w_ref[...], preferred_element_type=F32)
                out_ref[...] = out.astype(BF16)
            wide = flat_ref.shape[1]
            flat_ref[...] = whole_ref[:, index * wide : (index + 1) * wide]
            for k in range(slices // CORES // tiles):
                shard = CORES * (index * (slices // CORES // tiles) + k)
                begin = pl.multiple_of((shard + CORES - 1 - core) * size, size)
                send_ref[:, k * size : (k + 1) * size] = whole_ref[:, pl.ds(begin, size)]


def project(parts, weight, core, slices, flip):
    rows = sum(p.shape[0] for p in parts)
    depth, width = weight.shape[::-1] if flip else weight.shape
    tile = min(TILE, width // 2)
    tiles = width // tile
    each = lambda i, *_: (0, i)
    return call(
        functools.partial(project_kernel, flip, tiles, slices),
        (tiles,),
        core.reshape(1),
        [(p, fixed(p.shape)) if flip else resident(p) for p in parts]
        + [(weight, pl.BlockSpec((tile, depth), lambda i, *_: (i, 0)) if flip else pl.BlockSpec((depth, tile), each))],
        [
            ((rows, depth), BF16, pl.BlockSpec((rows, depth // tiles), each)),
            ((rows, depth // CORES), BF16, pl.BlockSpec((rows, depth // CORES // tiles), each)),
            ((rows, width), BF16, pl.BlockSpec((rows, tile), each)),
        ],
        2 * rows * depth * width,
        limit=((rows * (tiles + 3) // tiles + 2 * tile) + 2 * rows * flip) * depth * 2 // 2**20 + 5,
        scratch=[pltpu.VMEM((rows, depth), BF16)],
    )


def key_mask(flags_ref, doc, rows, total):
    row_block = lax.broadcasted_iota(jnp.int32, (rows, total), 0) // BLOCK
    col = lax.broadcasted_iota(jnp.int32, (rows, total), 1)
    offset = col // BLOCK - row_block
    seen = (offset == 1) | (col >= rows + 2 * BLOCK)
    window = col < rows + 2 * BLOCK
    for block in range(rows // BLOCK):
        here = (row_block == block) & window
        before = flags_ref[doc, 2 * block] == 1
        past = flags_ref[doc, 2 * block + 1] == 1
        seen = seen | (here & (offset == 0) & before) | (here & (offset == 2) & past)
    return seen


def joined(before_ref, own_ref, after_ref, glob_ref, head, shift):
    cols = slice(head * HDIM, (head + 1) * HDIM)
    side = slice(shift + head * HDIM, shift + (head + 1) * HDIM)
    return jnp.concatenate(
        [before_ref[:, side], own_ref[:, cols], after_ref[:, side], glob_ref[:, cols]], 0
    )


def attention_kernel(
    flags_ref, q_ref, k_ref, v_ref, before_ref, after_ref, gk_ref, gv_ref, do_ref,
    ctx_ref, dq_ref, dk_ref, dv_ref, dbefore_ref, dafter_ref, mine_ref, other_ref,
):
    rows, width = q_ref.shape
    total = rows + 2 * BLOCK + gk_ref.shape[0]
    doc = pl.program_id(0)
    seen = key_mask(flags_ref, doc, rows, total)
    first_core = flags_ref[doc, 2 * (rows // BLOCK)] == 0
    heads = range(width // HDIM)
    cols = [slice(head * HDIM, (head + 1) * HDIM) for head in heads]
    keys = [joined(before_ref, k_ref, after_ref, gk_ref, head, 0) for head in heads]
    values = [joined(before_ref, v_ref, after_ref, gv_ref, head, width) for head in heads]
    scores = [contract_cols(q_ref[:, cols[h]], keys[h]) * HDIM**-0.5 for h in heads]
    dweights = [contract_cols(do_ref[:, cols[h]], values[h]) for h in heads]
    scores = [jnp.where(seen, s, LOW) for s in scores]
    tops = [s.max(-1, keepdims=True) for s in scores]
    grown = [jnp.exp(scores[h] - tops[h]) for h in heads]
    sums = [g.sum(-1, keepdims=True) for g in grown]
    weights = [grown[h] / sums[h] for h in heads]
    deltas = [(weights[h] * dweights[h]).sum(-1, keepdims=True) for h in heads]
    weights_b = [w.astype(BF16) for w in weights]
    for h in heads:
        ctx_ref[:, cols[h]] = jnp.dot(weights_b[h], values[h], preferred_element_type=F32).astype(BF16)
    dvalues = [contract_rows(weights_b[h], do_ref[:, cols[h]]) for h in heads]
    dscores = [
        (weights[h] * (dweights[h] - deltas[h]) * HDIM**-0.5).astype(BF16) for h in heads
    ]
    for h in heads:
        dq_ref[:, cols[h]] = jnp.dot(dscores[h], keys[h], preferred_element_type=F32).astype(BF16)
    dkeys = [contract_rows(dscores[h], q_ref[:, cols[h]]) for h in heads]
    for h in heads:
        for own_ref, shift, grads in ((dk_ref, 0, dkeys[h]), (dv_ref, width, dvalues[h])):
            side = slice(shift + h * HDIM, shift + (h + 1) * HDIM)
            own_ref[:, cols[h]] = grads[BLOCK : rows + BLOCK]
            dbefore_ref[:, side] = grads[:BLOCK].astype(BF16)
            dafter_ref[:, side] = grads[rows + BLOCK : rows + 2 * BLOCK].astype(BF16)
        gk, gv = dkeys[h][rows + 2 * BLOCK :], dvalues[h][rows + 2 * BLOCK :]
        mine_ref[:, cols[h]] = jnp.where(first_core, gk, gv).astype(BF16)
        other_ref[:, cols[h]] = jnp.where(first_core, gv, gk).astype(BF16)


def by_doc(rows, width):
    return pl.BlockSpec((rows, width), lambda doc, *unused: (doc, 0))


def attention(kernel, docs, flags, operands, out_rows, flops, free):
    return call(
        kernel,
        (docs,),
        flags,
        [(a, by_doc(a.shape[0] // docs, a.shape[1])) for a in operands],
        [((docs * rows, width), dtype, by_doc(rows, width)) for rows, width, dtype in out_rows],
        flops,
        free=free,
    )


def finish_kernel(
    core_ref, dk_ref, dv_ref, ctx_ref, before_ref, after_ref, keys_ref, values_ref
):
    rows, width = dk_ref.shape
    values_ref[:, :width] = ctx_ref[...]
    for own_ref, shift, out_ref, to in ((dk_ref, 0, keys_ref, 0), (dv_ref, width, values_ref, width)):
        side, cols = slice(shift, shift + width), slice(to, to + width)
        out_ref[:BLOCK, cols] = (own_ref[:BLOCK] + before_ref[:, side].astype(F32)).astype(BF16)
        if rows > 2 * BLOCK:
            out_ref[BLOCK : rows - BLOCK, cols] = own_ref[BLOCK : rows - BLOCK].astype(BF16)
        out_ref[rows - BLOCK :, cols] = (own_ref[rows - BLOCK :] + after_ref[:, side].astype(F32)).astype(BF16)


def whole_kernel(
    core_ref, dk_ref, dv_ref, before_ref, after_ref, gk_ref, gv_ref, sel_ref, k_ref, v_ref
):
    rows, width = dk_ref.shape
    for own_ref, glob_ref, shift, out_ref in ((dk_ref, gk_ref, 0, k_ref), (dv_ref, gv_ref, width, v_ref)):
        total = own_ref[...] + contract_rows(sel_ref[...], glob_ref[...])
        side = slice(shift, shift + width)
        out_ref[:BLOCK] = (total[:BLOCK] + before_ref[:, side].astype(F32)).astype(BF16)
        if rows > 2 * BLOCK:
            out_ref[BLOCK : rows - BLOCK] = total[BLOCK : rows - BLOCK].astype(BF16)
        out_ref[rows - BLOCK :] = (total[rows - BLOCK :] + after_ref[:, side].astype(F32)).astype(BF16)


def transposed(value):
    return value.astype(F32).T.astype(value.dtype)


def terms_kernel(core_ref, c_ref, csib_ref, x_ref, xsib_ref, g_ref, gsib_ref, out_ref, turned_ref):
    rows, width = g_ref.shape[0], g_ref.shape[1] // 2
    size = x_ref.shape[1]

    @pl.when(pl.program_id(0) == 0)
    def _():
        turned_ref[:, :rows] = transposed(g_ref[...])
        turned_ref[:, rows:] = transposed(gsib_ref[...])

    for k, (own_ref, sib_ref) in enumerate(((c_ref, csib_ref), (x_ref, xsib_ref))):
        both = jnp.concatenate([own_ref[...], sib_ref[...]], 0)
        out = jnp.dot(turned_ref[k * width : (k + 1) * width], both, preferred_element_type=F32)
        out_ref[0, :, k * size : (k + 1) * size] = out.astype(BF16)


def chip_terms(cots, tokens, grads, core, slices):
    rows, depth = cots[0].shape
    width = grads.shape[1] // 2
    size, chips = depth // slices, slices // CORES
    own = pl.BlockSpec((rows, size), lambda z, c: (0, CORES * z + c[0]))
    other = pl.BlockSpec((rows, size), lambda z, c: (0, z))
    return call(
        terms_kernel,
        (chips,),
        core.reshape(1),
        [
            (cots[0], own),
            (cots[1], other),
            (tokens[0], own),
            (tokens[1], other),
            (grads, fixed(grads.shape)),
            (swap(grads, "seq", 1), fixed(grads.shape)),
        ],
        [((chips, width, 2 * size), BF16, pl.BlockSpec((1, width, 2 * size), lambda z, c: (z, 0, 0)))],
        8 * rows * size * chips * width,
        limit=24,
        scratch=[pltpu.VMEM((2 * width, 2 * rows), BF16)],
    )[0]


def line_schedule(count):
    return [
        {
            c: ("all", c - step) if step <= c else ("sum", count + c - step)
            for c in range(count - 1)
        }
        for step in range(count)
    ]


def pieces_kernel(count, table_ref, right_ref, left_ref, *refs):
    for way, (own_ref, out_ref) in enumerate(((right_ref, refs[-2]), (left_ref, refs[-1]))):
        is_sum, begins = table_ref[3 * way + 1] == 1, table_ref[3 * way + 2] == 1
        begin = 0
        for came_ref in refs[way * count : (way + 1) * count]:
            here = slice(begin, begin + came_ref.shape[1])
            begin += came_ref.shape[1]
            own, came = own_ref[0, :, here], came_ref[...]
            added = (own.astype(F32) + came.astype(F32)).astype(BF16)
            out_ref[:, here] = jnp.where(is_sum, jnp.where(begins, own, added), came)


def lookup(place, values):
    result = jnp.int32(values[0])
    for k, value in enumerate(values[1:], 1):
        result = jnp.where(place == k, jnp.int32(value), result)
    return result


class Line:
    def __init__(self, shape, chip, chips):
        self.partial, self.chip, self.chips, self.shape = None, chip, chips, shape
        self.schedule = line_schedule(chips)
        self.values, self.firsts, self.received = [], [], []

    def begin(self, value):
        self.values.append(value)
        self.firsts.append(self.move((value, value)))

    def join(self):
        self.rows, self.wide = self.values[0].shape[0], sum(v.shape[1] for v in self.values)
        self.size = tuple(max(a, b) for a, b in zip((self.rows, self.wide), self.shape))
        self.received.append(tuple(self.fit(jnp.concatenate(way, 1)) for way in zip(*self.firsts)))

    def fit(self, value):
        missing = [(0, want - have) for want, have in zip(self.size, value.shape)]
        return jnp.pad(value, missing) if any(m for _, m in missing) else value

    def place(self, sign):
        return self.chip if sign > 0 else self.chips - 1 - self.chip

    def pieces(self):
        chosen, pieces, table = self.schedule[len(self.received)], [], []
        count = self.chips
        plain = len(self.received) == 1 and self.size == self.shape == (self.rows, self.wide)
        for way, sign in enumerate((1, -1)):
            place = self.place(sign)
            sums = [int(chosen.get(c, ("", 0))[0] == "sum") for c in range(count)]
            which = [chosen.get(c, ("", c))[1] for c in range(count)]
            to = lookup(place, which)
            to = to if sign > 0 else count - 1 - to
            if plain:
                table += [to, lookup(place, sums), (place == 0).astype(jnp.int32)]
                continue
            own = self.fit(lax.dynamic_index_in_dim(self.partial, to, 0, keepdims=False))
            before = self.received[-1][way]
            added = (own.astype(F32) + before.astype(F32)).astype(BF16)
            pieces.append(jnp.where(lookup(place, sums) == 1, jnp.where(place == 0, own, added), before))
        if not plain:
            return pieces
        arrived = [list(way) for way in zip(*self.firsts)]
        rows, wide = self.size
        part = rows // 4
        return call(
            functools.partial(pieces_kernel, len(arrived[0])),
            (4,),
            jnp.stack(table),
            [(self.partial, pl.BlockSpec((1, part, wide), lambda i, t, at=at: (t[at], i * t[at + 1], 0))) for at in (0, 3)]
            + [
                (a, pl.BlockSpec((part, a.shape[1]), lambda i, t, at=at: (i * (1 - t[at + 1] * t[at + 2]), 0)))
                for at, way in zip((0, 3), arrived)
                for a in way
            ],
            [((rows, wide), BF16, pl.BlockSpec((part, wide), lambda i, *_: (i, 0)))] * 2,
            0,
            space=jax.ShapeDtypeStruct,
            free=range(2, 8),
        )

    def move(self, pieces):
        count, got = self.chips, []
        for piece, sign in zip(pieces, (1, -1)):
            pairs = [
                (c * CORES + b, (c + sign) * CORES + b)
                for c in (range(count - 1) if sign > 0 else range(count - 1, 0, -1))
                for b in range(CORES)
            ]
            got.append(lax.ppermute(piece, "seq", pairs))
        return tuple(got)

    def send(self, pieces):
        self.received.append(self.move(pieces))

    def step(self):
        self.send(self.pieces())

    def gathered(self, columns, sums, positions, core):
        rows, wide = self.rows, self.wide
        slots, grads = [jnp.int32(0)], [self.values]
        for t in range(self.chips - 1):
            for way, sign in enumerate((1, -1)):
                values = [-1] * self.chips
                for c, (kind, which) in self.schedule[t].items():
                    if kind == "all":
                        values[c + 1] = (sign * (c + 1 - which)) % self.chips
                slots.append(lookup(self.place(sign), values))
                if t:
                    grads.append([self.received[t][way][:rows, :wide]])
                else:
                    grads.append([first[way] for first in self.firsts])
        height, width = columns[0].shape[1], wide // 2
        size = height // CORES
        once = lambda a: (a, pl.BlockSpec(a.shape, lambda *_: (0,) * a.ndim, pipeline_mode=pl.Buffered(1)))
        return call(
            functools.partial(gathered_kernel, len(columns), [len(g) for g in grads]),
            (1,),
            jnp.stack(slots + [core, self.chip]),
            [once(a) for a in columns + list(sums) + [positions] + sum(grads, [])],
            [
                ((size, 3 * width), F32, fixed((size, 3 * width))),
            ]
            + [((size, width), BF16, fixed((size, width)))] * 3,
            4 * height * width * len(grads) * rows,
            limit=44,
            scratch=[pltpu.VMEM((height, 3 * width), F32)],
        )


def final_kernel(chip_ref, *refs):
    sums, (mine_ref, *others), (q_ref, k_ref, v_ref, o_ref) = refs[:6], refs[6:10], refs[10:]
    width = q_ref.shape[1]
    for refs, out_ref in ((sums[0::2], o_ref), (sums[1::2], None)):
        total = refs[0][0].astype(F32) + refs[1][...].astype(F32) + refs[2][...].astype(F32)
        if out_ref is not None:
            out_ref[...] = total
    q_ref[...] = mine_ref[:, :width] + others[0][...].astype(F32)
    k_ref[...] = mine_ref[:, width : 2 * width] + others[1][...].astype(F32)
    v_ref[...] = mine_ref[:, 2 * width :] + others[2][...].astype(F32) + total.T


def final_sums(line, mine, others, width):
    rows, size, part = line.partial.shape[1], mine.shape[0], 128
    skip = size // part
    ins = [
        (line.partial, pl.BlockSpec((1, part, size), lambda i, c: (c[0], i, 0))),
        (line.partial, pl.BlockSpec((1, rows, part), lambda i, c: (c[0], 0, skip + i))),
    ]
    for came in line.received[-1]:
        ins.append((came, pl.BlockSpec((part, size), lambda i, *_: (i, 0))))
        ins.append((came, pl.BlockSpec((rows, part), lambda i, *_: (0, skip + i))))
    by_part = lambda wide: pl.BlockSpec((part, wide), lambda i, *_: (i, 0))
    return call(
        final_kernel,
        (skip,),
        line.chip.reshape(1),
        ins + [(a, by_part(a.shape[1])) for a in (mine, *others)],
        [((size, width), F32, by_part(width))] * 3 + [((rows, size), F32, by_part(size))],
        0,
        limit=32,
        free=range(2, 10),
    )


def columns_to_chips(block, chip, chips):
    turned = block.T
    size = turned.shape[0] // chips
    pieces = []
    for s in range(chips):
        piece = lax.dynamic_slice_in_dim(turned, lax.rem(chip + s, chips) * size, size, 0)
        if s:
            pairs = [
                (c * CORES + b, (c + s) % chips * CORES + b) for c in range(chips) for b in range(CORES)
            ]
            piece = lax.ppermute(piece, "seq", pairs)
        pieces.append(piece)
    return pieces


def gathered_kernel(docs, groups, slots_ref, *refs):
    x_refs, (gk_ref, gv_ref, positions_ref), g_refs = refs[:docs], refs[docs : docs + 3], refs[docs + 3 : -5]
    mine_ref, *other_refs, total_ref = refs[-5:]
    width = gk_ref.shape[1]
    sent = 2 * width
    chips, _, rows = x_refs[0].shape
    core, chip = slots_ref[len(groups)], slots_ref[len(groups) + 1]

    def add(slot, group, first):
        x = jnp.concatenate([x_ref[slot] for x_ref in x_refs], 1)
        begin = 0
        for g_ref in group:
            here = slice(begin, begin + g_ref.shape[1])
            term = jnp.dot(x, g_ref[...], preferred_element_type=F32)
            total_ref[:, here] = term if first else total_ref[:, here] + term
            begin += g_ref.shape[1]

    begin = 0
    for k, count in enumerate(groups):
        group = g_refs[begin : begin + count]
        begin += count
        if k == 0:
            add(0, group, True)
            continue

        @pl.when(slots_ref[k] >= 0)
        def _(k=k, group=group):
            add(slots_ref[k], group, False)

    globs = gk_ref.shape[0] // docs
    chosen = []
    for doc in range(docs):
        picked = None
        for slot in range(chips):
            begin = (lax.rem(chip + chips - slot, chips) * CORES + core) * rows
            place = begin + lax.broadcasted_iota(jnp.int32, (rows, globs), 0)
            onehot = (place == positions_ref[doc]).astype(F32).astype(BF16)
            part = jnp.dot(x_refs[doc][slot], onehot, preferred_element_type=F32)
            picked = part if picked is None else picked + part
        chosen.append(picked.astype(BF16))
    chosen = jnp.concatenate(chosen, 1)
    total_ref[:, sent - width : sent] += jnp.dot(chosen, gk_ref[...], preferred_element_type=F32)
    total_ref[:, sent:] = jnp.dot(chosen, gv_ref[...], preferred_element_type=F32)

    size = mine_ref.shape[0]
    mine_ref[...] = total_ref[pl.ds(pl.multiple_of(core * size, size), size)]
    other = total_ref[pl.ds(pl.multiple_of((CORES - 1 - core) * size, size), size)]
    for k, other_ref in enumerate(other_refs):
        other_ref[...] = other[:, k * width : (k + 1) * width].astype(BF16)


def tokens_kernel(places, core_ref, q_ref, k_ref, v_ref, wq_ref, wk_ref, wv_ref, *out_refs):
    total = None
    for g_ref, w_ref in ((q_ref, wq_ref), (k_ref, wk_ref), (v_ref, wv_ref)):
        term = contract_cols(w_ref[...], g_ref[...])
        total = term if total is None else total + term
    total = total.T.astype(BF16)
    for (begin, count), out_ref in zip(places, out_refs):
        out_ref[...] = total[begin : begin + count]


def token_terms(docs, rows, grads, weights, core):
    depth, width = weights[0].shape
    tile = 512
    places = []
    for r in range(docs):
        halves = 2 if bin(r).count("1") > 1 else 1
        places += [(r * rows + k * rows // halves, rows // halves) for k in range(halves)]
    pieces = call(
        functools.partial(tokens_kernel, places),
        (depth // tile,),
        core.reshape(1),
        [(g, fixed(g.shape)) for g in grads]
        + [(w, pl.BlockSpec((tile, width), lambda i, *_: (i, 0))) for w in weights],
        [((count, depth), BF16, pl.BlockSpec((count, tile), lambda i, *_: (0, i))) for _, count in places],
        6 * docs * rows * depth * width,
        limit=24,
    )
    terms = {r: [] for r in range(docs)}
    for (begin, _), piece in zip(places, pieces):
        terms[begin // rows].append(piece)
    return terms


def on_device(tokens, cotangent, w_query, w_key, w_value, w_output, global_pos, pattern):
    docs = lax.axis_size("fsdp")
    n_seq = lax.axis_size("seq")
    seq = lax.axis_index("seq")
    core, chip, chips = lax.rem(seq, CORES), lax.div(seq, CORES), n_seq // CORES
    rows, model_width = tokens.shape[1:]
    width = w_query.shape[1]
    block_count = rows // BLOCK
    order = lax.axis_index("fsdp") ^ jnp.arange(docs, dtype=jnp.int32)
    global_pos = jnp.take(global_pos, order, axis=0)
    pattern = jnp.take(pattern, order, axis=0)
    globs = global_pos.shape[1]

    index = seq * block_count + jnp.arange(block_count, dtype=jnp.int32)
    inside = jnp.stack([index > 0, index < block_count * n_seq - 1], -1)
    flags = ((pattern == 1) & inside[None]).astype(jnp.int32).reshape(docs, 2 * block_count)
    flags = jnp.concatenate([flags, jnp.broadcast_to(core, (docs, 1))], 1)
    selector = (
        (global_pos[:, :, None] - seq * rows == jnp.arange(rows, dtype=jnp.int32)[None, None, :])
        .astype(BF16)
        .reshape(docs * globs, rows)
    )

    block, cot = tokens[0], cotangent[0]
    pieces = columns_to_chips(block, chip, chips)
    near, selector, flags = phase((near_blocks(block, "fsdp"), selector, flags))
    whole = {0: block, **near}
    far = far_blocks({r: cut(v) for r, v in whole.items()}, "fsdp")
    parts = [p for r in range(docs) for p in ([whole[r]] if r in whole else far[r])]
    parts, cot_halves, pieces = phase((parts, cut(cot), pieces))

    near_a = near_blocks(cot_halves[0], "fsdp")
    keys, values, first, last, mine, other = project_keys(
        parts, selector, w_key, w_value, core, docs
    )
    keys, values, first, last, mine, other, near_a, cot_b, parts, pieces = phase(
        (keys, values, first, last, mine, other, near_a, cot_halves[1], parts, pieces)
    )

    near_b = near_blocks(cot_b, "fsdp")
    glob = sum_first(mine, other, chip)
    flat, for_sibling, query = project(parts, w_query, core, n_seq, False)
    glob, near_b, flat, query, for_sibling, first, last, pieces = phase(
        (glob, near_b, flat, query, for_sibling, first, last, pieces)
    )
    halves = {0: (cot_halves[0], cot_b)}
    halves.update({r: (near_a[r], near_b[r]) for r in near_a})
    far = far_blocks(halves, "fsdp")
    glob = sum(sum_second(glob, chips))
    columns = jnp.stack(pieces)
    glob, far, first, last, for_sibling, columns = phase((glob, far, first, last, for_sibling, columns))
    glob = sum_third(glob, chip)
    past = lax.ppermute(first, "seq", shift_pairs(n_seq, -1))
    before = lax.ppermute(last, "seq", shift_pairs(n_seq, 1))
    cot_parts = [cot] + [p for r in range(1, docs) for p in far[r]]
    grads_flat, grads_for_sibling, grad_ctx = project(cot_parts, w_output, core, n_seq, True)
    glob, grads_flat, grads_for_sibling, grad_ctx, columns, for_sibling, past, before = phase(
        (glob, grads_flat, grads_for_sibling, grad_ctx, columns, for_sibling, past, before)
    )
    glob_k, glob_v = sum_last(glob, core)
    glob_k, glob_v, grads_for_sibling, for_sibling = phase(
        (glob_k, glob_v, grads_for_sibling, for_sibling)
    )
    grads_sibling = swap(grads_for_sibling, "seq", 1)
    tokens_sibling = swap(for_sibling, "seq", 1)

    near_columns = near_blocks(columns, "fsdp")
    context, grad_q, dkey, dvalue, dbefore, dafter, dmine, dother = attention(
        attention_kernel,
        docs,
        flags,
        [query, keys, values, before, past, glob_k, glob_v, grad_ctx],
        [
            (rows, width, BF16),
            (rows, width, BF16),
            (rows, width, F32),
            (rows, width, F32),
            (BLOCK, 2 * width, BF16),
            (BLOCK, 2 * width, BF16),
            (globs, width, BF16),
            (globs, width, BF16),
        ],
        14 * docs * rows * (rows + 2 * BLOCK + globs) * width,
        free=(3, 4, 5, 6),
    )

    (context, grad_q, dkey, dvalue, dbefore, dafter, dmine, dother), columns, grads_sibling, tokens_sibling = phase(
        ((context, grad_q, dkey, dvalue, dbefore, dafter, dmine, dother), columns, grads_sibling, tokens_sibling)
    )

    line = Line((width, 2 * model_width // n_seq), chip, chips)
    kept, given = halves_of(dmine + swap(dother, "seq", 1), chip & 1)
    kept, given, dbefore, dafter, grad_q = phase((kept, given, dbefore, dafter, grad_q))
    given = swap(given, "seq", CORES)
    from_after = lax.ppermute(dbefore, "seq", shift_pairs(n_seq, -1))
    from_before = lax.ppermute(dafter, "seq", shift_pairs(n_seq, 1))
    line.begin(grad_q)
    dglob, context = phase((kept + given, context))
    dglob, came = sum_second(dglob, chips)
    to_gather, to_scatter = call(
        finish_kernel,
        (docs,),
        core.reshape(1),
        [
            (a, by_doc(a.shape[0] // docs, a.shape[1]))
            for a in (dkey, dvalue, context, from_before, from_after)
        ],
        [((docs * rows, k * width), BF16, by_doc(rows, k * width)) for k in (1, 2)],
        4 * docs * rows * globs * width,
        free=(3, 4),
    )
    to_gather, to_scatter, columns, near_columns, came, line.firsts = phase(
        (to_gather, to_scatter, columns, near_columns, came, line.firsts)
    )
    dglob = dglob + came

    line.begin(to_gather)
    line.partial = chip_terms((grads_flat, grads_sibling), (flat, tokens_sibling), to_scatter, core, n_seq)
    line.firsts, line.partial, dglob = phase((line.firsts, line.partial, dglob))
    line.join()
    line.step()
    dglob = sum_third(dglob, chip)
    whole = {0: columns, **near_columns}
    far = far_blocks({r: cut(v) for r, v in whole.items()}, "fsdp")
    sums = sum_last(dglob, core)
    grad_k, grad_v = call(
        whole_kernel,
        (docs,),
        core.reshape(1),
        [
            (a, by_doc(a.shape[0] // docs, a.shape[1]))
            for a in (dkey, dvalue, from_before, from_after, *sums, selector)
        ],
        [((docs * rows, width), BF16, by_doc(rows, width))] * 2,
        4 * docs * rows * globs * width,
        free=(4, 5),
    )
    terms = token_terms(docs, rows, (grad_q, grad_k, grad_v), (w_query, w_key, w_value), core)
    line.received, sums, far, whole, terms = phase((line.received, sums, far, whole, terms))
    scatter, bits = BlockScatter(terms, "fsdp"), docs.bit_length() - 1
    pieces, far, own_terms = phase((line.pieces(), far, scatter.own()))
    scatter.put_own(own_terms)
    line.send(pieces)
    columns = [whole[r] if r in whole else jnp.concatenate(far[r], 0) for r in range(docs)]
    scatter.send(bits)
    scatter.collapse()
    line.received, sums, columns, scatter.terms = phase((line.received, sums, columns, scatter.terms))
    while len(line.received) < len(line.schedule) - 1:
        line.step()
    pieces, sums, columns, own_terms = phase((line.pieces(), sums, columns, scatter.own()))
    scatter.put_own(own_terms)
    line.send(pieces)
    for weight in range(bits - 1, 0, -1):
        scatter.send(weight)
    mine, *others = line.gathered(columns, sums, global_pos[:, None, :], core)
    grad_tokens, others = phase((scatter.total().astype(BF16)[None], others))
    others = [swap(other, "seq", 1) for other in others]
    line.received, mine, others = phase((line.received, mine, others))
    grad_query, grad_key, grad_value, grad_output = final_sums(line, mine, others, width)
    return (grad_tokens, grad_query, grad_key, grad_value, grad_output)


def solution(mesh):
    in_specs = (
        P("fsdp", "seq", None),
        P("fsdp", "seq", None),
        P(None, "fsdp"),
        P(None, "fsdp"),
        P(None, "fsdp"),
        P("fsdp", None),
        P(),
        P(None, "seq", None),
    )
    out_specs = (
        P("fsdp", "seq", None),
        P("seq", "fsdp"),
        P("seq", "fsdp"),
        P("seq", "fsdp"),
        P("fsdp", "seq"),
    )
    return jax.shard_map(
        on_device, mesh=mesh, in_specs=in_specs, out_specs=out_specs, check_vma=False
    )
```
